32 devices in a mesh: row: 2 (over core), sector: 4 (over y, x), inst: 4 (over z).
Axes of the slice: x: 2, y: 2, z: 4, core: 2. Of those that a mesh axis runs over, the one named last changes fastest.
Arguments:
- state: bfloat16 [2, 4, 8, 5, 16384], P('row', 'sector', 'inst'), may hold values from -6 to 6
- gradients: bfloat16 [2, 4, 8, 15, 16384], P('row', 'sector', 'inst'), may hold values from -6 to 6
- jacobian: bfloat16 [2, 4, 8, 25, 16384], P('row', 'sector', 'inst'), may hold values from -2.5 to 2.5
- pseudo_step: float32 [2, 4, 8, 16384], P('row', 'sector', 'inst'), may hold values from 0.25 to 0.6
- frequency: float32 [2], P('row'), may hold values from 0.1 to 0.4
- donor_cells: int32 [2, 4, 8, 128], P('row', 'sector'), may hold values from 0 to 16383
- block_count: int32 [2, 4], P('row', 'sector'), may hold values from 2 to 8, as said below
- matching: int32 [2, 4, 8, 8], P('row', 'sector', 'inst'), may hold values from 0 to 3, as said below
- target_cells: int32 [2, 4, 8, 4, 2, 128], P('row', 'sector', 'inst'), may hold values from 0 to 16383
- interp_weights: bfloat16 [2, 4, 8, 4, 2, 128, 128], P('row', 'sector', 'inst'), may hold values from -0.5 to 0.5
- face_offsets: float32 [2, 4, 8, 4, 2, 3, 128], P('row', 'sector', 'inst'), may hold values from -3 to 3
Outputs:
- updated: float32 [2, 4, 8, 5, 16384], P('row', 'sector', 'inst')
The draws below stay inside these ranges and needn't reach their ends.
Inputs may be any that keep to these rules, and one draw needn't show every extreme that they name: `block_count`: every row has a sector with exactly 8 live blocks; live blocks of a sector are its first ones. `matching`: among the live blocks of one sector and instance, at most 2 name the same receiving sector; for every donor row and instance some receiving sector is named by exactly 2 live blocks of every donor sector.
All inputs are finite; a program needn't handle non-finite values.
Results may differ from the reference program's by a relative error of at most 0.0029.
Values may be sent and summed in bfloat16 or wider, within the bound.
A program may use at most 128 MiB of HBM per device.

```python
import math
import jax
import jax.numpy as jnp
from jax import lax

NV = 5
FROWS = 20
BLK = 128
CAP = 2
SWEEPS = 6
CELLS = 16384
ROWS = 2
NSEC = 4
NT = 8
MAXB = 8


def routing_tables(key):
    shifts = jax.random.randint(jax.random.fold_in(key, 11), (ROWS, NSEC), 0, 4).astype(jnp.int32)
    live_count = jnp.maximum(2, jnp.right_shift(jnp.full((ROWS, NSEC), MAXB, jnp.int32), shifts))
    busiest = jax.random.randint(jax.random.fold_in(key, 13), (ROWS, 1), 0, NSEC)
    live_count = jnp.where(jnp.arange(NSEC, dtype=jnp.int32)[None, :] == busiest, MAXB, live_count).astype(jnp.int32)
    perm_keys = jax.random.split(jax.random.fold_in(key, 17), ROWS * NSEC * NT)
    orders = jax.vmap(lambda one_key: jax.random.permutation(one_key, MAXB))(perm_keys)
    orders = orders.astype(jnp.int32).reshape(ROWS, NSEC, NT, MAXB)
    count_all = jnp.broadcast_to(live_count[:, :, None], (ROWS, NSEC, NT))
    first_pick = jax.random.randint(jax.random.fold_in(key, 19), (ROWS, NSEC, NT), 0, count_all)
    second_step = jax.random.randint(jax.random.fold_in(key, 23), (ROWS, NSEC, NT), 1, count_all)
    second_pick = (first_pick + second_step) % count_all
    first_value = jnp.take_along_axis(orders, first_pick[..., None], axis=-1)[..., 0]
    paired_value = jnp.bitwise_xor(first_value, 1)
    inverse = jnp.argsort(orders, axis=-1).astype(jnp.int32)
    holder = jnp.take_along_axis(inverse, paired_value[..., None], axis=-1)[..., 0]
    second_value = jnp.take_along_axis(orders, second_pick[..., None], axis=-1)[..., 0]
    positions = jnp.arange(MAXB, dtype=jnp.int32)
    orders = jnp.where(positions == second_pick[..., None], paired_value[..., None], jnp.where(positions == holder[..., None], second_value[..., None], orders))
    receiver = jax.random.randint(jax.random.fold_in(key, 29), (ROWS, 1, NT), 0, NSEC)
    base = receiver - first_value // 2
    matching = (base[..., None] + orders // 2) % NSEC
    return (live_count, matching.astype(jnp.int32))


def draw_block_count(key, part):
    live_count, matching = routing_tables(key)
    return live_count


def draw_matching(key, part):
    live_count, matching = routing_tables(key)
    return matching


def place_ends(drawn, rng, least, high):
    spot = [jax.random.randint(jax.random.fold_in(rng, axis), (), 0, length) for axis, length in enumerate(drawn.shape)]
    main_axis = drawn.shape.index(max(drawn.shape))
    next_to = spot[:main_axis] + [(spot[main_axis] + 1) % drawn.shape[main_axis]] + spot[main_axis + 1:]
    return drawn.at[tuple(spot)].set(least).at[tuple(next_to)].set(high)


def levels(stream_key, dims, cuts, least, top_value):
    def one(dim, blocks):
        heights = jax.random.uniform(jax.random.fold_in(jax.random.fold_in(stream_key, 6), dim), (blocks,), jnp.float32, least / len(cuts), top_value / len(cuts))
        return jnp.repeat(jnp.exp(heights), dims[dim] // blocks).reshape((-1,) + (1,) * (len(dims) - dim - 1))

    gain = one(*cuts[0])
    for cut in cuts[1:]:
        gain = gain * one(*cut)
    return gain


def bell_draw(stream_key, shape, deviation, most, cuts=(), kind=jnp.bfloat16):
    entries = jax.random.normal(stream_key, shape, jnp.float32) * deviation
    if len(cuts) > 0:
        entries = levels(stream_key, shape, cuts, -0.22, 0.18) * entries
    return jnp.clip(entries, min=-most, max=most).astype(kind)


def setup_inputs(seed: int = 0) -> dict:
    arg_keys = jax.random.split(jax.random.key(seed), 12)
    return {
        "state": bell_draw(arg_keys[0], (ROWS, NSEC, NT, NV, CELLS), 1.0, 6.0, ((0, 2), (1, 4), (2, 4))),
        "gradients": bell_draw(arg_keys[1], (ROWS, NSEC, NT, 3 * NV, CELLS), 1.0, 6.0, ((0, 2), (1, 4), (2, 4))),
        "jacobian": bell_draw(arg_keys[2], (ROWS, NSEC, NT, NV * NV, CELLS), NV ** -0.5, 2.5, ((0, 2), (1, 4), (2, 4))),
        "pseudo_step": jnp.clip(jnp.exp(math.log(0.6) - 0.8754688 * jax.random.uniform(arg_keys[3], (ROWS, NSEC, NT, CELLS), jnp.float32) ** levels(arg_keys[3], (ROWS, NSEC, NT, CELLS), ((0, 2), (1, 4), (2, 4)), -0.2, 0.2)), 0.25, 0.6),
        "frequency": jnp.clip(jnp.exp(math.log(0.4) - 1.3862944 * jax.random.uniform(arg_keys[4], (ROWS,), jnp.float32) ** levels(arg_keys[4], (ROWS,), ((0, 2),), -0.2, 0.2)), 0.1, 0.4),
        "donor_cells": place_ends(jax.random.randint(arg_keys[5], (ROWS, NSEC, MAXB, BLK), 0, CELLS), jax.random.fold_in(arg_keys[5], 1), 0, CELLS - 1).astype(jnp.int32),
        "block_count": draw_block_count(jax.random.fold_in(arg_keys[11], 71), 0),
        "matching": draw_matching(jax.random.fold_in(arg_keys[11], 71), 0),
        "target_cells": place_ends(jax.random.randint(arg_keys[8], (ROWS, NSEC, NT, NSEC, CAP, BLK), 0, CELLS), jax.random.fold_in(arg_keys[8], 1), 0, CELLS - 1).astype(jnp.int32),
        "interp_weights": bell_draw(arg_keys[9], (ROWS, NSEC, NT, NSEC, CAP, BLK, BLK), BLK ** -0.5, 0.5, ((0, 2), (1, 4), (2, 4))),
        "face_offsets": bell_draw(arg_keys[10], (ROWS, NSEC, NT, NSEC, CAP, 3, BLK), 0.5, 3.0, ((0, 2), (1, 4), (2, 4)), jnp.float32),
    }


def spectral_block(row_first, row_count, col_first, col_count, period):
    row_index = row_first + jnp.arange(row_count, dtype=jnp.int32)[:, None]
    col_index = col_first + jnp.arange(col_count, dtype=jnp.int32)[None, :]
    index_gap = row_index - col_index
    diagonal_mask = index_gap == 0
    safe_gap = jnp.where(diagonal_mask, 1, index_gap)
    phase_angle = safe_gap.astype(jnp.float32) * (math.pi / period)
    sign_flip = (1 - 2 * (jnp.abs(index_gap) % 2)).astype(jnp.float32)
    cot_entry = 0.5 * sign_flip * jnp.cos(phase_angle) / jnp.sin(phase_angle)
    return jnp.where(diagonal_mask, jnp.zeros_like(cot_entry), cot_entry)


def slot_ranks(receiver, is_live, sectors):
    one_hot = (receiver[..., None] == jnp.arange(sectors, dtype=jnp.int32)).astype(jnp.int32)
    one_hot = one_hot * is_live[..., None].astype(jnp.int32)
    earlier = jnp.cumsum(one_hot, axis=-2) - one_hot
    return jnp.sum(earlier * one_hot, axis=-1).astype(jnp.int32)


def couple_faces(mixed, offsets, nvar):
    face_values = mixed[..., :nvar, :]
    face_slopes = mixed[..., nvar:, :].reshape(mixed.shape[:-2] + (3, nvar, mixed.shape[-1]))
    return face_values + jnp.sum(offsets[..., :, None, :] * face_slopes, axis=-3)


def apply_jacobian(jacobi_wide, vector):
    return jnp.sum(jacobi_wide.astype(jnp.float32) * vector[:, None], axis=2)


def reference(state, gradients, jacobian, pseudo_step, frequency, donor_cells, block_count, matching, target_cells, interp_weights, face_offsets):
    row_ids = jnp.arange(ROWS, dtype=jnp.int32)[:, None, None, None]
    sector_ids = jnp.arange(NSEC, dtype=jnp.int32)[None, :, None, None]
    inst_ids = jnp.arange(NT, dtype=jnp.int32)[None, None, :, None]
    shape_four = matching.shape
    is_live = jnp.arange(MAXB, dtype=jnp.int32)[None, None, None, :] < block_count[:, :, None, None]
    is_live = jnp.broadcast_to(is_live, shape_four)
    slot_rank = slot_ranks(matching, is_live, NSEC)
    source = jnp.concatenate([state, gradients], axis=3)

    def gather_faces(source_column, cells_column):
        picked = jnp.take(source_column, cells_column.reshape(-1), axis=2)
        return picked.reshape(NT, FROWS, MAXB, BLK).transpose(0, 2, 1, 3)

    face_rows = jax.vmap(jax.vmap(gather_faces))(source, donor_cells)
    face_rows = jnp.where(is_live[..., None, None], face_rows, jnp.zeros_like(face_rows))
    arrived = jnp.zeros((ROWS, NSEC, NT, NSEC, CAP, FROWS, BLK), jnp.bfloat16)
    arrived = arrived.at[
        jnp.broadcast_to(1 - row_ids, shape_four),
        matching,
        jnp.broadcast_to(inst_ids, shape_four),
        jnp.broadcast_to(sector_ids, shape_four),
        slot_rank,
    ].add(face_rows)
    dmatrix = spectral_block(0, NT, 0, NT, NT)
    rotation_all = jnp.repeat(frequency, NSEC)

    def spread_faces(faces_one, targets_one):
        flat_faces = faces_one.transpose(2, 0, 1, 3).reshape(NV, -1)
        return jnp.zeros((NV, CELLS), flat_faces.dtype).at[:, targets_one.reshape(-1)].add(flat_faces)

    def one_column(packed):
        flow, jacobi, pseudo, rotation, arrived_col, weights_col, offsets_col, targets_col = packed
        flow_wide = flow.astype(jnp.float32)
        jacobi_wide = jacobi.reshape(NT, NV, NV, CELLS)
        spectral = rotation * jnp.einsum("tu,uvc->tvc", dmatrix, flow_wide, precision=lax.Precision.HIGHEST)
        mixed = jnp.einsum("tskqf,tskfg->tskqg", arrived_col.astype(jnp.float32), weights_col.astype(jnp.float32))
        coupled = couple_faces(mixed, offsets_col, NV)
        coupling = jax.vmap(spread_faces)(coupled, targets_col)
        residual = apply_jacobian(jacobi_wide, flow_wide) + spectral - coupling
        increment = -pseudo[:, None, :] * residual
        for sweep in range(SWEEPS):
            increment = -pseudo[:, None, :] * (residual + apply_jacobian(jacobi_wide, increment))
        return flow_wide + increment

    columns = ROWS * NSEC
    packed_all = (
        state.reshape((columns,) + state.shape[2:]),
        jacobian.reshape((columns,) + jacobian.shape[2:]),
        pseudo_step.reshape((columns,) + pseudo_step.shape[2:]),
        rotation_all,
        arrived.reshape((columns,) + arrived.shape[2:]),
        interp_weights.reshape((columns,) + interp_weights.shape[2:]),
        face_offsets.reshape((columns,) + face_offsets.shape[2:]),
        target_cells.reshape((columns,) + target_cells.shape[2:]),
    )
    result = lax.map(one_column, packed_all)
    return result.reshape(ROWS, NSEC, NT, NV, CELLS)
```

```python
import functools
import math

import jax
import jax.numpy as jnp
import numpy as np
from jax import lax
from jax.experimental import pallas as pl
from jax.experimental.pallas import tpu as pltpu
from jax.sharding import PartitionSpec as P

SWEEPS = 6
LANES = 128
WIDE = 256
SLOT_ROWS = 32
STAGE_ROWS = 48
MESH = pl.DeviceIdType.MESH
VMEM_LIMIT = 48 * 1024 * 1024


def spectral_matrix(period):
    index = np.arange(period)
    gap = index[:, None] - index[None, :]
    safe_gap = np.where(gap == 0, 1, gap)
    angle = safe_gap * (math.pi / period)
    entry = 0.5 * (1 - 2 * (np.abs(gap) % 2)) * np.cos(angle) / np.sin(angle)
    return np.where(gap == 0, 0.0, entry).astype(np.float32)


def one_hot_rows(index_row):
    rows = lax.broadcasted_iota(jnp.int32, (WIDE, index_row.shape[1]), 0)
    return jnp.where(rows == index_row, 1.0, 0.0).astype(jnp.bfloat16)


def gather_kernel(capacity, count_ref, matching_ref, donor_ref, state_ref, grad_ref, send_ref, source):
    inst_local, nvar, cells = state_ref.shape
    nslope = grad_ref.shape[1]
    slots = donor_ref.shape[0]
    sectors = send_ref.shape[0]
    columns = sectors * capacity * LANES
    part = min(columns, 1024)
    source[...] = jnp.zeros_like(source)
    for t in range(inst_local):
        source[t, 0:nvar, :] = state_ref[t]
        source[t, 16 : 16 + nslope, :] = grad_ref[t]
    block_id = lax.broadcasted_iota(jnp.int32, (1, columns), 1) // LANES
    block_sector = block_id // capacity
    block_rank = block_id % capacity
    group = 4
    for t in range(inst_local):
        index_row = jnp.full((1, columns), -1, jnp.int32)
        seen = jnp.zeros((1, columns), jnp.int32)
        for b in range(slots):
            target = jnp.where(b < count_ref[0], matching_ref[t, b], -1)
            hit = block_sector == target
            cells_row = jnp.concatenate([donor_ref[b : b + 1, :]] * (columns // LANES), axis=1)
            index_row = jnp.where(hit & (seen == block_rank), cells_row, index_row)
            seen = seen + jnp.where(hit, 1, 0)
        for first in range(0, columns, part):
            piece = index_row[:, first : first + part]
            high = piece >> 8
            hot = one_hot_rows(piece & (WIDE - 1))

            def step(g, total):
                rows = [
                    source[t, :, pl.ds(pl.multiple_of((g * group + j) * WIDE, WIDE), WIDE)]
                    for j in range(group)
                ]
                picked = jnp.dot(
                    jnp.concatenate(rows, axis=0), hot, preferred_element_type=jnp.float32
                )
                for j in range(group):
                    mine = picked[j * SLOT_ROWS : (j + 1) * SLOT_ROWS]
                    total = total + jnp.where(high == g * group + j, mine, 0.0)
                return total

            total = lax.fori_loop(
                0, cells // WIDE // group, step, jnp.zeros((SLOT_ROWS, part), jnp.float32)
            ).astype(jnp.bfloat16)
            for j in range(part // LANES):
                d, k = divmod(first // LANES + j, capacity)
                send_ref[d, (t * capacity + k) * SLOT_ROWS : (t * capacity + k + 1) * SLOT_ROWS, :] = (
                    total[:, j * LANES : (j + 1) * LANES]
                )


def exchange_kernel(sectors, insts, send_ref, state_ref, recv_ref, all_ref, fs, fr, ss, sr, own):
    row = lax.axis_index("row")
    sector = lax.axis_index("sector")
    inst = lax.axis_index("inst")
    barrier = pltpu.get_barrier_semaphore()
    for d in range(sectors):
        pl.semaphore_signal(barrier, inc=1, device_id=(1 - row, d, inst), device_id_type=MESH)
    for step in range(1, insts):
        pl.semaphore_signal(
            barrier, inc=1, device_id=(row, sector, (inst + step) % insts), device_id_type=MESH
        )
    pl.semaphore_wait(barrier, sectors + insts - 1)
    copies = []
    for step in range(1, insts):
        peer = (inst + step) % insts
        copies.append(
            pltpu.make_async_remote_copy(
                src_ref=state_ref,
                dst_ref=all_ref.at[inst],
                send_sem=ss.at[step - 1],
                recv_sem=sr.at[step - 1],
                device_id=(row, sector, peer),
                device_id_type=MESH,
            )
        )
    for step in range(sectors):
        peer = (sector + step) % sectors
        copies.append(
            pltpu.make_async_remote_copy(
                src_ref=send_ref.at[peer],
                dst_ref=recv_ref.at[sector],
                send_sem=fs.at[step],
                recv_sem=fr.at[step],
                device_id=(1 - row, peer, inst),
                device_id_type=MESH,
            )
        )
    for copy in copies:
        copy.start()
    mine = pltpu.make_async_copy(state_ref, all_ref.at[inst], own)
    mine.start()
    mine.wait()
    for copy in copies:
        copy.wait()


def update_kernel(
    dmat_ref, freq_ref, recv_ref, weights_ref, offsets_ref, targets_ref, all_ref, state_ref,
    jac_ref, pseudo_ref, out_ref, faces, coupling, stage, out_stage,
):
    inst_local, nvar, cells = state_ref.shape
    sectors, capacity = targets_ref.shape[1:3]
    insts = all_ref.shape[0]
    first_row = lax.axis_index("inst") * inst_local
    rotation = freq_ref[0]
    faces[...] = jnp.zeros_like(faces)
    group = 4
    for t in range(inst_local):
        target_rows = []
        for m in range(sectors):
            for k in range(capacity):
                slot = t * capacity + k
                column = (m * capacity + k) * LANES
                mixed = jnp.dot(
                    recv_ref[m, slot * SLOT_ROWS : (slot + 1) * SLOT_ROWS, :],
                    weights_ref[t, m, k],
                    preferred_element_type=jnp.float32,
                )
                value = mixed[0:nvar]
                for d in range(3):
                    begin = 16 + d * nvar
                    value = value + offsets_ref[t, m, k, d : d + 1, :] * mixed[begin : begin + nvar]
                upper = value.astype(jnp.bfloat16).astype(jnp.float32)
                faces[t, 0:nvar, column : column + LANES] = upper
                faces[t, 8 : 8 + nvar, column : column + LANES] = value - upper
                target_rows.append(targets_ref[t, m, k : k + 1, :])
        target_row = jnp.concatenate(target_rows, axis=1)
        high = target_row >> 8
        hot = one_hot_rows(target_row & (WIDE - 1))

        def spread(g, carry):
            face_values = faces[t]
            rows = [jnp.where(high == g * group + j, face_values, 0.0) for j in range(group)]
            placed = lax.dot_general(
                jnp.concatenate(rows, axis=0).astype(jnp.bfloat16),
                hot,
                (((1,), (1,)), ((), ())),
                preferred_element_type=jnp.float32,
            )
            for j in range(group):
                begin = pl.multiple_of((g * group + j) * WIDE, WIDE)
                coupling[t, :, pl.ds(begin, WIDE)] = (
                    placed[j * 16 : j * 16 + 8] + placed[j * 16 + 8 : j * 16 + 16]
                )
            return carry

        lax.fori_loop(0, cells // WIDE // group, spread, 0)

    chunk = 8 * LANES
    for t in range(inst_local):
        coefs = [
            [dmat_ref[first_row + t, i * inst_local + u] * rotation for u in range(inst_local)]
            for i in range(insts)
        ]

        def relax(c, carry):
            window = pl.ds(pl.multiple_of(c * chunk, chunk), chunk)
            jac = jac_ref[t, :, window].astype(jnp.float32)
            flow = state_ref[t, :, window].astype(jnp.float32)
            pseudo = pseudo_ref[t : t + 1, window]
            rest = -coupling[t, 0:nvar, window]
            for i in range(insts):
                for u in range(inst_local):
                    rest = rest + coefs[i][u] * all_ref[i, u, :, window].astype(jnp.float32)
            for j in range(8):
                lanes = slice(j * LANES, (j + 1) * LANES)
                at = j * STAGE_ROWS
                stage[at : at + nvar * nvar, :] = jac[:, lanes]
                stage[at + 32 : at + 32 + nvar, :] = rest[:, lanes]
                stage[at + 40 : at + 40 + nvar, :] = flow[:, lanes]
                stage[at + 46 : at + 47, :] = pseudo[:, lanes]

            def row(r):
                return stage[pl.ds(r, 8, stride=STAGE_ROWS), :]

            matrix = [[row(v * nvar + w) for w in range(nvar)] for v in range(nvar)]
            base = [row(40 + v) for v in range(nvar)]
            shift = -row(46)

            def apply(start, vector):
                result = []
                for v in range(nvar):
                    acc = start[v]
                    for w in range(nvar):
                        acc = acc + matrix[v][w] * vector[w]
                    result.append(acc)
                return result

            residual = apply([row(32 + v) for v in range(nvar)], base)
            increment = [shift * value for value in residual]
            for sweep in range(SWEEPS):
                increment = [shift * value for value in apply(residual, increment)]
            for v in range(nvar):
                out_stage[pl.ds(v, 8, stride=8), :] = base[v] + increment[v]
            for j in range(8):
                begin = pl.multiple_of(c * chunk + j * LANES, LANES)
                out_ref[t, :, pl.ds(begin, LANES)] = out_stage[j * 8 : j * 8 + nvar, :]
            return carry

        lax.fori_loop(0, cells // chunk, relax, 0)


def body(
    state,
    gradients,
    jacobian,
    pseudo_step,
    frequency,
    donor_cells,
    block_count,
    matching,
    target_cells,
    interp_weights,
    face_offsets,
):
    flow = state[0, 0]
    inst_local, nvar, cells = flow.shape
    sectors = lax.axis_size("sector")
    insts = lax.axis_size("inst")
    capacity = target_cells.shape[4]
    columns = sectors * capacity * LANES
    vmem = pl.BlockSpec(memory_space=pltpu.VMEM)
    smem = pl.BlockSpec(memory_space=pltpu.SMEM)
    hbm = pl.BlockSpec(memory_space=pl.ANY)
    packet = jax.ShapeDtypeStruct((sectors, inst_local * capacity * SLOT_ROWS, LANES), jnp.bfloat16)
    send = pl.pallas_call(
        functools.partial(gather_kernel, capacity),
        out_shape=packet,
        in_specs=[smem, smem, vmem, vmem, vmem],
        out_specs=vmem,
        scratch_shapes=[pltpu.VMEM((inst_local, SLOT_ROWS, cells), jnp.bfloat16)],
        compiler_params=pltpu.CompilerParams(vmem_limit_bytes=VMEM_LIMIT),
    )(block_count.reshape(1), matching[0, 0], donor_cells[0, 0], flow, gradients[0, 0])
    recv, everything = pl.pallas_call(
        functools.partial(exchange_kernel, sectors, insts),
        out_shape=(packet, jax.ShapeDtypeStruct((insts,) + flow.shape, flow.dtype)),
        in_specs=[hbm, hbm],
        out_specs=(hbm, hbm),
        scratch_shapes=[
            pltpu.SemaphoreType.DMA((sectors,)),
            pltpu.SemaphoreType.DMA((sectors,)),
            pltpu.SemaphoreType.DMA((insts - 1,)),
            pltpu.SemaphoreType.DMA((insts - 1,)),
            pltpu.SemaphoreType.DMA,
        ],
        compiler_params=pltpu.CompilerParams(collective_id=0, has_side_effects=True),
    )(send, flow)
    dmat = jnp.asarray(spectral_matrix(inst_local * insts))
    result = pl.pallas_call(
        update_kernel,
        out_shape=jax.ShapeDtypeStruct(flow.shape, jnp.float32),
        in_specs=[smem, smem] + [vmem] * 8,
        out_specs=vmem,
        scratch_shapes=[
            pltpu.VMEM((inst_local, 16, columns), jnp.float32),
            pltpu.VMEM((inst_local, 8, cells), jnp.float32),
            pltpu.VMEM((8 * STAGE_ROWS, LANES), jnp.float32),
            pltpu.VMEM((64, LANES), jnp.float32),
        ],
        compiler_params=pltpu.CompilerParams(vmem_limit_bytes=VMEM_LIMIT),
    )(
        dmat,
        frequency,
        recv,
        interp_weights[0, 0],
        face_offsets[0, 0],
        target_cells[0, 0],
        everything,
        flow,
        jacobian[0, 0],
        pseudo_step[0, 0],
    )
    return result[None, None]


def solution(mesh):
    placed = (
        P("row", "sector", "inst", None, None),
        P("row", "sector", "inst", None, None),
        P("row", "sector", "inst", None, None),
        P("row", "sector", "inst", None),
        P("row"),
        P("row", "sector", None, None),
        P("row", "sector"),
        P("row", "sector", "inst", None),
        P("row", "sector", "inst", None, None, None),
        P("row", "sector", "inst", None, None, None, None),
        P("row", "sector", "inst", None, None, None, None),
    )
    return jax.shard_map(
        body,
        mesh=mesh,
        in_specs=placed,
        out_specs=P("row", "sector", "inst", None, None),
        check_vma=False,
    )
```

```python
import functools
import math

import jax
import jax.numpy as jnp
import numpy as np
from jax import lax
from jax.experimental import pallas as pl
from jax.experimental.pallas import tpu as pltpu
from jax.sharding import PartitionSpec as P

SWEEPS = 6
LANES = 128
WIDE = 256
SLOT_ROWS = 32
STAGE_ROWS = 48
MESH = pl.DeviceIdType.MESH
VMEM_LIMIT = 48 * 1024 * 1024


def spectral_matrix(period):
    index = np.arange(period)
    gap = index[:, None] - index[None, :]
    safe_gap = np.where(gap == 0, 1, gap)
    angle = safe_gap * (math.pi / period)
    entry = 0.5 * (1 - 2 * (np.abs(gap) % 2)) * np.cos(angle) / np.sin(angle)
    return np.where(gap == 0, 0.0, entry).astype(np.float32)


def one_hot_rows(index_row):
    rows = lax.broadcasted_iota(jnp.int32, (WIDE, index_row.shape[1]), 0)
    return jnp.where(rows == index_row, 1.0, 0.0).astype(jnp.bfloat16)


def gather_kernel(capacity, count_ref, matching_ref, donor_ref, state_ref, grad_ref, send_ref, source):
    inst_local, nvar, cells = state_ref.shape
    nslope = grad_ref.shape[1]
    slots = donor_ref.shape[0]
    sectors = send_ref.shape[0]
    columns = sectors * capacity * LANES
    part = min(columns, 1024)
    source[...] = jnp.zeros_like(source)
    for t in range(inst_local):
        source[t, 0:nvar, :] = state_ref[t]
        source[t, 16 : 16 + nslope, :] = grad_ref[t]
    block_id = lax.broadcasted_iota(jnp.int32, (1, columns), 1) // LANES
    block_sector = block_id // capacity
    block_rank = block_id % capacity
    group = 4
    for t in range(inst_local):
        index_row = jnp.full((1, columns), -1, jnp.int32)
        seen = jnp.zeros((1, columns), jnp.int32)
        for b in range(slots):
            target = jnp.where(b < count_ref[0], matching_ref[t, b], -1)
            hit = block_sector == target
            cells_row = jnp.concatenate([donor_ref[b : b + 1, :]] * (columns // LANES), axis=1)
            index_row = jnp.where(hit & (seen == block_rank), cells_row, index_row)
            seen = seen + jnp.where(hit, 1, 0)
        for first in range(0, columns, part):
            piece = index_row[:, first : first + part]
            high = piece >> 8
            hot = one_hot_rows(piece & (WIDE - 1))

            def step(g, total):
                rows = [
                    source[t, :, pl.ds(pl.multiple_of((g * group + j) * WIDE, WIDE), WIDE)]
                    for j in range(group)
                ]
                picked = jnp.dot(
                    jnp.concatenate(rows, axis=0), hot, preferred_element_type=jnp.float32
                )
                for j in range(group):
                    mine = picked[j * SLOT_ROWS : (j + 1) * SLOT_ROWS]
                    total = total + jnp.where(high == g * group + j, mine, 0.0)
                return total

            total = lax.fori_loop(
                0, cells // WIDE // group, step, jnp.zeros((SLOT_ROWS, part), jnp.float32)
            ).astype(jnp.bfloat16)
            for j in range(part // LANES):
                d, k = divmod(first // LANES + j, capacity)
                send_ref[d, (t * capacity + k) * SLOT_ROWS : (t * capacity + k + 1) * SLOT_ROWS, :] = (
                    total[:, j * LANES : (j + 1) * LANES]
                )


def exchange_kernel(sectors, insts, send_ref, state_ref, recv_ref, all_ref, fs, fr, ss, sr, own):
    row = lax.axis_index("row")
    sector = lax.axis_index("sector")
    inst = lax.axis_index("inst")
    barrier = pltpu.get_barrier_semaphore()
    for d in range(sectors):
        pl.semaphore_signal(barrier, inc=1, device_id=(1 - row, d, inst), device_id_type=MESH)
    for step in range(1, insts):
        pl.semaphore_signal(
            barrier, inc=1, device_id=(row, sector, (inst + step) % insts), device_id_type=MESH
        )
    pl.semaphore_wait(barrier, sectors + insts - 1)
    copies = []
    for step in range(1, insts):
        peer = (inst + step) % insts
        copies.append(
            pltpu.make_async_remote_copy(
                src_ref=state_ref,
                dst_ref=all_ref.at[inst],
                send_sem=ss.at[step - 1],
                recv_sem=sr.at[step - 1],
                device_id=(row, sector, peer),
                device_id_type=MESH,
            )
        )
    for step in range(sectors):
        peer = (sector + step) % sectors
        copies.append(
            pltpu.make_async_remote_copy(
                src_ref=send_ref.at[peer],
                dst_ref=recv_ref.at[sector],
                send_sem=fs.at[step],
                recv_sem=fr.at[step],
                device_id=(1 - row, peer, inst),
                device_id_type=MESH,
            )
        )
    for copy in copies:
        copy.start()
    mine = pltpu.make_async_copy(state_ref, all_ref.at[inst], own)
    mine.start()
    mine.wait()
    for copy in copies:
        copy.wait()


def update_kernel(
    dmat_ref, freq_ref, recv_ref, weights_ref, offsets_ref, targets_ref, all_ref, state_ref,
    jac_ref, pseudo_ref, out_ref, faces, coupling, stage, out_stage,
):
    inst_local, nvar, cells = state_ref.shape
    sectors, capacity = targets_ref.shape[1:3]
    insts = all_ref.shape[0]
    first_row = lax.axis_index("inst") * inst_local
    rotation = freq_ref[0]
    faces[...] = jnp.zeros_like(faces)
    group = 4
    for t in range(inst_local):
        target_rows = []
        for m in range(sectors):
            for k in range(capacity):
                slot = t * capacity + k
                column = (m * capacity + k) * LANES
                mixed = jnp.dot(
                    recv_ref[m, slot * SLOT_ROWS : (slot + 1) * SLOT_ROWS, :],
                    weights_ref[t, m, k],
                    preferred_element_type=jnp.float32,
                )
                value = mixed[0:nvar]
                for d in range(3):
                    begin = 16 + d * nvar
                    value = value + offsets_ref[t, m, k, d : d + 1, :] * mixed[begin : begin + nvar]
                upper = value.astype(jnp.bfloat16).astype(jnp.float32)
                faces[t, 0:nvar, column : column + LANES] = upper
                faces[t, 8 : 8 + nvar, column : column + LANES] = value - upper
                target_rows.append(targets_ref[t, m, k : k + 1, :])
        target_row = jnp.concatenate(target_rows, axis=1)
        high = target_row >> 8
        hot = one_hot_rows(target_row & (WIDE - 1))

        def spread(g, carry):
            face_values = faces[t]
            rows = [jnp.where(high == g * group + j, face_values, 0.0) for j in range(group)]
            placed = lax.dot_general(
                jnp.concatenate(rows, axis=0).astype(jnp.bfloat16),
                hot,
                (((1,), (1,)), ((), ())),
                preferred_element_type=jnp.float32,
            )
            for j in range(group):
                begin = pl.multiple_of((g * group + j) * WIDE, WIDE)
                coupling[t, :, pl.ds(begin, WIDE)] = (
                    placed[j * 16 : j * 16 + 8] + placed[j * 16 + 8 : j * 16 + 16]
                )
            return carry

        lax.fori_loop(0, cells // WIDE // group, spread, 0)

    chunk = 8 * LANES
    for t in range(inst_local):
        coefs = [
            [dmat_ref[first_row + t, i * inst_local + u] * rotation for u in range(inst_local)]
            for i in range(insts)
        ]

        def relax(c, carry):
            window = pl.ds(pl.multiple_of(c * chunk, chunk), chunk)
            jac = jac_ref[t, :, window].astype(jnp.float32)
            flow = state_ref[t, :, window].astype(jnp.float32)
            pseudo = pseudo_ref[t : t + 1, window]
            position = lax.broadcasted_iota(jnp.int32, (inst_local, chunk), 0)
            mixture = jnp.zeros((nvar, inst_local, chunk), jnp.float32)
            for i in range(insts):
                factor = jnp.zeros((inst_local, chunk), jnp.float32)
                for u in range(inst_local):
                    factor = jnp.where(position == u, coefs[i][u], factor)
                mixture = mixture + factor[None] * all_ref[i, :, :, window].astype(jnp.float32)
            rest = jnp.sum(mixture, axis=1) - coupling[t, 0:nvar, window]
            for j in range(8):
                lanes = slice(j * LANES, (j + 1) * LANES)
                at = j * STAGE_ROWS
                stage[at : at + nvar * nvar, :] = jac[:, lanes]
                stage[at + 32 : at + 32 + nvar, :] = rest[:, lanes]
                stage[at + 40 : at + 40 + nvar, :] = flow[:, lanes]
                stage[at + 46 : at + 47, :] = pseudo[:, lanes]

            def row(r):
                return stage[pl.ds(r, 8, stride=STAGE_ROWS), :]

            matrix = [[row(v * nvar + w) for w in range(nvar)] for v in range(nvar)]
            base = [row(40 + v) for v in range(nvar)]
            shift = -row(46)

            def apply(start, vector):
                result = []
                for v in range(nvar):
                    acc = start[v]
                    for w in range(nvar):
                        acc = acc + matrix[v][w] * vector[w]
                    result.append(acc)
                return result

            residual = apply([row(32 + v) for v in range(nvar)], base)
            increment = [shift * value for value in residual]
            for sweep in range(SWEEPS):
                increment = [shift * value for value in apply(residual, increment)]
            for v in range(nvar):
                out_stage[pl.ds(v, 8, stride=8), :] = base[v] + increment[v]
            for j in range(8):
                begin = pl.multiple_of(c * chunk + j * LANES, LANES)
                out_ref[t, :, pl.ds(begin, LANES)] = out_stage[j * 8 : j * 8 + nvar, :]
            return carry

        lax.fori_loop(0, cells // chunk, relax, 0)


def body(
    state,
    gradients,
    jacobian,
    pseudo_step,
    frequency,
    donor_cells,
    block_count,
    matching,
    target_cells,
    interp_weights,
    face_offsets,
):
    flow = state[0, 0]
    inst_local, nvar, cells = flow.shape
    sectors = lax.axis_size("sector")
    insts = lax.axis_size("inst")
    capacity = target_cells.shape[4]
    columns = sectors * capacity * LANES
    vmem = pl.BlockSpec(memory_space=pltpu.VMEM)
    smem = pl.BlockSpec(memory_space=pltpu.SMEM)
    hbm = pl.BlockSpec(memory_space=pl.ANY)
    packet = jax.ShapeDtypeStruct((sectors, inst_local * capacity * SLOT_ROWS, LANES), jnp.bfloat16)
    send = pl.pallas_call(
        functools.partial(gather_kernel, capacity),
        out_shape=packet,
        in_specs=[smem, smem, vmem, vmem, vmem],
        out_specs=vmem,
        scratch_shapes=[pltpu.VMEM((inst_local, SLOT_ROWS, cells), jnp.bfloat16)],
        compiler_params=pltpu.CompilerParams(vmem_limit_bytes=VMEM_LIMIT),
    )(block_count.reshape(1), matching[0, 0], donor_cells[0, 0], flow, gradients[0, 0])
    compact = flow.transpose(1, 0, 2)
    recv, everything = pl.pallas_call(
        functools.partial(exchange_kernel, sectors, insts),
        out_shape=(packet, jax.ShapeDtypeStruct((insts,) + compact.shape, flow.dtype)),
        in_specs=[hbm, hbm],
        out_specs=(hbm, hbm),
        scratch_shapes=[
            pltpu.SemaphoreType.DMA((sectors,)),
            pltpu.SemaphoreType.DMA((sectors,)),
            pltpu.SemaphoreType.DMA((insts - 1,)),
            pltpu.SemaphoreType.DMA((insts - 1,)),
            pltpu.SemaphoreType.DMA,
        ],
        compiler_params=pltpu.CompilerParams(collective_id=0, has_side_effects=True),
    )(send, compact)
    dmat = jnp.asarray(spectral_matrix(inst_local * insts))
    result = pl.pallas_call(
        update_kernel,
        out_shape=jax.ShapeDtypeStruct(flow.shape, jnp.float32),
        in_specs=[smem, smem] + [vmem] * 8,
        out_specs=vmem,
        scratch_shapes=[
            pltpu.VMEM((inst_local, 16, columns), jnp.float32),
            pltpu.VMEM((inst_local, 8, cells), jnp.float32),
            pltpu.VMEM((8 * STAGE_ROWS, LANES), jnp.float32),
            pltpu.VMEM((64, LANES), jnp.float32),
        ],
        compiler_params=pltpu.CompilerParams(vmem_limit_bytes=VMEM_LIMIT),
    )(
        dmat,
        frequency,
        recv,
        interp_weights[0, 0],
        face_offsets[0, 0],
        target_cells[0, 0],
        everything,
        flow,
        jacobian[0, 0],
        pseudo_step[0, 0],
    )
    return result[None, None]


def solution(mesh):
    placed = (
        P("row", "sector", "inst", None, None),
        P("row", "sector", "inst", None, None),
        P("row", "sector", "inst", None, None),
        P("row", "sector", "inst", None),
        P("row"),
        P("row", "sector", None, None),
        P("row", "sector"),
        P("row", "sector", "inst", None),
        P("row", "sector", "inst", None, None, None),
        P("row", "sector", "inst", None, None, None, None),
        P("row", "sector", "inst", None, None, None, None),
    )
    return jax.shard_map(
        body,
        mesh=mesh,
        in_specs=placed,
        out_specs=P("row", "sector", "inst", None, None),
        check_vma=False,
    )
```

```python
import functools
import math

import jax
import jax.numpy as jnp
import numpy as np
from jax import lax
from jax.experimental import pallas as pl
from jax.experimental.pallas import tpu as pltpu
from jax.sharding import PartitionSpec as P

SWEEPS = 6
LANES = 128
WIDE = 256
SLOT_ROWS = 32
STAGE_ROWS = 48
MESH = pl.DeviceIdType.MESH
VMEM_LIMIT = 48 * 1024 * 1024


def spectral_matrix(period):
    index = np.arange(period)
    gap = index[:, None] - index[None, :]
    safe_gap = np.where(gap == 0, 1, gap)
    angle = safe_gap * (math.pi / period)
    entry = 0.5 * (1 - 2 * (np.abs(gap) % 2)) * np.cos(angle) / np.sin(angle)
    return np.where(gap == 0, 0.0, entry).astype(np.float32)


def one_hot_rows(index_row):
    rows = lax.broadcasted_iota(jnp.int32, (WIDE, index_row.shape[1]), 0)
    return jnp.where(rows == index_row, 1.0, 0.0).astype(jnp.bfloat16)


def gather_faces(capacity, count_ref, matching_ref, donor_ref, state_ref, grad_ref, send_ref, source):
    inst_local, nvar, cells = state_ref.shape
    nslope = grad_ref.shape[1]
    slots = donor_ref.shape[0]
    sectors = send_ref.shape[0]
    columns = sectors * capacity * LANES
    part = min(columns, 1024)
    source[...] = jnp.zeros_like(source)
    for t in range(inst_local):
        source[t, 0:nvar, :] = state_ref[t]
        source[t, 16 : 16 + nslope, :] = grad_ref[t]
    block_id = lax.broadcasted_iota(jnp.int32, (1, columns), 1) // LANES
    block_sector = block_id // capacity
    block_rank = block_id % capacity
    group = 4
    for t in range(inst_local):
        index_row = jnp.full((1, columns), -1, jnp.int32)
        seen = jnp.zeros((1, columns), jnp.int32)
        for b in range(slots):
            target = jnp.where(b < count_ref[0], matching_ref[t, b], -1)
            hit = block_sector == target
            cells_row = jnp.concatenate([donor_ref[b : b + 1, :]] * (columns // LANES), axis=1)
            index_row = jnp.where(hit & (seen == block_rank), cells_row, index_row)
            seen = seen + jnp.where(hit, 1, 0)
        for first in range(0, columns, part):
            piece = index_row[:, first : first + part]
            high = piece >> 8
            hot = one_hot_rows(piece & (WIDE - 1))

            def step(g, total):
                rows = [
                    source[t, :, pl.ds(pl.multiple_of((g * group + j) * WIDE, WIDE), WIDE)]
                    for j in range(group)
                ]
                picked = jnp.dot(
                    jnp.concatenate(rows, axis=0), hot, preferred_element_type=jnp.float32
                )
                for j in range(group):
                    mine = picked[j * SLOT_ROWS : (j + 1) * SLOT_ROWS]
                    total = total + jnp.where(high == g * group + j, mine, 0.0)
                return total

            total = lax.fori_loop(
                0, cells // WIDE // group, step, jnp.zeros((SLOT_ROWS, part), jnp.float32)
            ).astype(jnp.bfloat16)
            for j in range(part // LANES):
                d, k = divmod(first // LANES + j, capacity)
                send_ref[d, (t * capacity + k) * SLOT_ROWS : (t * capacity + k + 1) * SLOT_ROWS, :] = (
                    total[:, j * LANES : (j + 1) * LANES]
                )


def exchange_kernel(
    sectors, insts, capacity, count_ref, matching_ref, donor_ref, flow_ref, grad_ref, state_ref,
    recv_ref, all_ref, source, send_ref, fs, fr, ss, sr, own,
):
    row = lax.axis_index("row")
    sector = lax.axis_index("sector")
    inst = lax.axis_index("inst")
    barrier = pltpu.get_barrier_semaphore()
    for d in range(sectors):
        pl.semaphore_signal(barrier, inc=1, device_id=(1 - row, d, inst), device_id_type=MESH)
    for step in range(1, insts):
        pl.semaphore_signal(
            barrier, inc=1, device_id=(row, sector, (inst + step) % insts), device_id_type=MESH
        )
    pl.semaphore_wait(barrier, sectors + insts - 1)
    copies = []
    for step in range(1, insts):
        peer = (inst + step) % insts
        copies.append(
            pltpu.make_async_remote_copy(
                src_ref=state_ref,
                dst_ref=all_ref.at[inst],
                send_sem=ss.at[step - 1],
                recv_sem=sr.at[step - 1],
                device_id=(row, sector, peer),
                device_id_type=MESH,
            )
        )
    for copy in copies:
        copy.start()
    mine = pltpu.make_async_copy(state_ref, all_ref.at[inst], own)
    mine.start()
    gather_faces(
        capacity, count_ref, matching_ref, donor_ref, flow_ref, grad_ref, send_ref, source
    )
    for step in range(sectors):
        peer = (sector + step) % sectors
        copy = pltpu.make_async_remote_copy(
            src_ref=send_ref.at[peer],
            dst_ref=recv_ref.at[sector],
            send_sem=fs.at[step],
            recv_sem=fr.at[step],
            device_id=(1 - row, peer, inst),
            device_id_type=MESH,
        )
        copy.start()
        copies.append(copy)
    mine.wait()
    for copy in copies:
        copy.wait()


def update_kernel(
    dmat_ref, freq_ref, recv_ref, weights_ref, offsets_ref, targets_ref, all_ref, state_ref,
    jac_ref, pseudo_ref, out_ref, faces, coupling, stage, out_stage,
):
    inst_local, nvar, cells = state_ref.shape
    sectors, capacity = targets_ref.shape[1:3]
    insts = all_ref.shape[0]
    first_row = lax.axis_index("inst") * inst_local
    rotation = freq_ref[0]
    faces[...] = jnp.zeros_like(faces)
    group = 4
    for t in range(inst_local):
        target_rows = []
        for m in range(sectors):
            for k in range(capacity):
                slot = t * capacity + k
                column = (m * capacity + k) * LANES
                mixed = jnp.dot(
                    recv_ref[m, slot * SLOT_ROWS : (slot + 1) * SLOT_ROWS, :],
                    weights_ref[t, m, k],
                    preferred_element_type=jnp.float32,
                )
                value = mixed[0:nvar]
                for d in range(3):
                    begin = 16 + d * nvar
                    value = value + offsets_ref[t, m, k, d : d + 1, :] * mixed[begin : begin + nvar]
                upper = value.astype(jnp.bfloat16).astype(jnp.float32)
                faces[t, 0:nvar, column : column + LANES] = upper
                faces[t, 8 : 8 + nvar, column : column + LANES] = value - upper
                target_rows.append(targets_ref[t, m, k : k + 1, :])
        target_row = jnp.concatenate(target_rows, axis=1)
        high = target_row >> 8
        hot = one_hot_rows(target_row & (WIDE - 1))

        def spread(g, carry):
            face_values = faces[t]
            rows = [jnp.where(high == g * group + j, face_values, 0.0) for j in range(group)]
            placed = lax.dot_general(
                jnp.concatenate(rows, axis=0).astype(jnp.bfloat16),
                hot,
                (((1,), (1,)), ((), ())),
                preferred_element_type=jnp.float32,
            )
            for j in range(group):
                begin = pl.multiple_of((g * group + j) * WIDE, WIDE)
                coupling[t, :, pl.ds(begin, WIDE)] = (
                    placed[j * 16 : j * 16 + 8] + placed[j * 16 + 8 : j * 16 + 16]
                )
            return carry

        lax.fori_loop(0, cells // WIDE // group, spread, 0)

    chunk = 8 * LANES
    for t in range(inst_local):
        coefs = [
            [dmat_ref[first_row + t, i * inst_local + u] * rotation for u in range(inst_local)]
            for i in range(insts)
        ]

        def relax(c, carry):
            window = pl.ds(pl.multiple_of(c * chunk, chunk), chunk)
            jac = jac_ref[t, :, window].astype(jnp.float32)
            flow = state_ref[t, :, window].astype(jnp.float32)
            pseudo = pseudo_ref[t : t + 1, window]
            position = lax.broadcasted_iota(jnp.int32, (inst_local, chunk), 0)
            mixture = jnp.zeros((nvar, inst_local, chunk), jnp.float32)
            for i in range(insts):
                factor = jnp.zeros((inst_local, chunk), jnp.float32)
                for u in range(inst_local):
                    factor = jnp.where(position == u, coefs[i][u], factor)
                mixture = mixture + factor[None] * all_ref[i, :, :, window].astype(jnp.float32)
            rest = jnp.sum(mixture, axis=1) - coupling[t, 0:nvar, window]
            for j in range(8):
                lanes = slice(j * LANES, (j + 1) * LANES)
                at = j * STAGE_ROWS
                stage[at : at + nvar * nvar, :] = jac[:, lanes]
                stage[at + 32 : at + 32 + nvar, :] = rest[:, lanes]
                stage[at + 40 : at + 40 + nvar, :] = flow[:, lanes]
                stage[at + 46 : at + 47, :] = pseudo[:, lanes]

            def row(r):
                return stage[pl.ds(r, 8, stride=STAGE_ROWS), :]

            matrix = [[row(v * nvar + w) for w in range(nvar)] for v in range(nvar)]
            base = [row(40 + v) for v in range(nvar)]
            shift = -row(46)

            def apply(start, vector):
                result = []
                for v in range(nvar):
                    acc = start[v]
                    for w in range(nvar):
                        acc = acc + matrix[v][w] * vector[w]
                    result.append(acc)
                return result

            residual = apply([row(32 + v) for v in range(nvar)], base)
            increment = [shift * value for value in residual]
            for sweep in range(SWEEPS):
                increment = [shift * value for value in apply(residual, increment)]
            for v in range(nvar):
                out_stage[pl.ds(v, 8, stride=8), :] = base[v] + increment[v]
            for j in range(8):
                begin = pl.multiple_of(c * chunk + j * LANES, LANES)
                out_ref[t, :, pl.ds(begin, LANES)] = out_stage[j * 8 : j * 8 + nvar, :]
            return carry

        lax.fori_loop(0, cells // chunk, relax, 0)


def body(
    state,
    gradients,
    jacobian,
    pseudo_step,
    frequency,
    donor_cells,
    block_count,
    matching,
    target_cells,
    interp_weights,
    face_offsets,
):
    flow = state[0, 0]
    inst_local, nvar, cells = flow.shape
    sectors = lax.axis_size("sector")
    insts = lax.axis_size("inst")
    capacity = target_cells.shape[4]
    columns = sectors * capacity * LANES
    vmem = pl.BlockSpec(memory_space=pltpu.VMEM)
    smem = pl.BlockSpec(memory_space=pltpu.SMEM)
    hbm = pl.BlockSpec(memory_space=pl.ANY)
    packet = jax.ShapeDtypeStruct((sectors, inst_local * capacity * SLOT_ROWS, LANES), jnp.bfloat16)
    compact = flow.transpose(1, 0, 2)
    recv, everything = pl.pallas_call(
        functools.partial(exchange_kernel, sectors, insts, capacity),
        out_shape=(packet, jax.ShapeDtypeStruct((insts,) + compact.shape, flow.dtype)),
        in_specs=[smem, smem, vmem, vmem, vmem, hbm],
        out_specs=(hbm, hbm),
        scratch_shapes=[
            pltpu.VMEM((inst_local, SLOT_ROWS, cells), jnp.bfloat16),
            pltpu.VMEM(packet.shape, packet.dtype),
            pltpu.SemaphoreType.DMA((sectors,)),
            pltpu.SemaphoreType.DMA((sectors,)),
            pltpu.SemaphoreType.DMA((insts - 1,)),
            pltpu.SemaphoreType.DMA((insts - 1,)),
            pltpu.SemaphoreType.DMA,
        ],
        compiler_params=pltpu.CompilerParams(
            collective_id=0, has_side_effects=True, vmem_limit_bytes=VMEM_LIMIT
        ),
    )(block_count.reshape(1), matching[0, 0], donor_cells[0, 0], flow, gradients[0, 0], compact)
    dmat = jnp.asarray(spectral_matrix(inst_local * insts))
    result = pl.pallas_call(
        update_kernel,
        out_shape=jax.ShapeDtypeStruct(flow.shape, jnp.float32),
        in_specs=[smem, smem] + [vmem] * 8,
        out_specs=vmem,
        scratch_shapes=[
            pltpu.VMEM((inst_local, 16, columns), jnp.float32),
            pltpu.VMEM((inst_local, 8, cells), jnp.float32),
            pltpu.VMEM((8 * STAGE_ROWS, LANES), jnp.float32),
            pltpu.VMEM((64, LANES), jnp.float32),
        ],
        compiler_params=pltpu.CompilerParams(vmem_limit_bytes=VMEM_LIMIT),
    )(
        dmat,
        frequency,
        recv,
        interp_weights[0, 0],
        face_offsets[0, 0],
        target_cells[0, 0],
        everything,
        flow,
        jacobian[0, 0],
        pseudo_step[0, 0],
    )
    return result[None, None]


def solution(mesh):
    placed = (
        P("row", "sector", "inst", None, None),
        P("row", "sector", "inst", None, None),
        P("row", "sector", "inst", None, None),
        P("row", "sector", "inst", None),
        P("row"),
        P("row", "sector", None, None),
        P("row", "sector"),
        P("row", "sector", "inst", None),
        P("row", "sector", "inst", None, None, None),
        P("row", "sector", "inst", None, None, None, None),
        P("row", "sector", "inst", None, None, None, None),
    )
    return jax.shard_map(
        body,
        mesh=mesh,
        in_specs=placed,
        out_specs=P("row", "sector", "inst", None, None),
        check_vma=False,
    )
```

```python
import functools
import math

import jax
import jax.numpy as jnp
import numpy as np
from jax import lax
from jax.experimental import pallas as pl
from jax.experimental.pallas import tpu as pltpu
from jax.sharding import PartitionSpec as P

SWEEPS = 6
LANES = 128
WIDE = 256
SLOT_ROWS = 32
STAGE_ROWS = 48
MESH = pl.DeviceIdType.MESH
VMEM_LIMIT = 48 * 1024 * 1024


def spectral_matrix(period):
    index = np.arange(period)
    gap = index[:, None] - index[None, :]
    safe_gap = np.where(gap == 0, 1, gap)
    angle = safe_gap * (math.pi / period)
    entry = 0.5 * (1 - 2 * (np.abs(gap) % 2)) * np.cos(angle) / np.sin(angle)
    return np.where(gap == 0, 0.0, entry).astype(np.float32)


def one_hot_rows(index_row):
    rows = lax.broadcasted_iota(jnp.int32, (WIDE, index_row.shape[1]), 0)
    return jnp.where(rows == index_row, 1.0, 0.0).astype(jnp.bfloat16)


def gather_faces(capacity, count_ref, matching_ref, donor_ref, state_ref, grad_ref, send_ref, source):
    inst_local, nvar, cells = state_ref.shape
    nslope = grad_ref.shape[1]
    slots = donor_ref.shape[0]
    sectors = send_ref.shape[0]
    columns = sectors * capacity * LANES
    part = min(columns, 1024)
    source[...] = jnp.zeros_like(source)
    for t in range(inst_local):
        source[t, 0:nvar, :] = state_ref[t]
        source[t, 16 : 16 + nslope, :] = grad_ref[t]
    block_id = lax.broadcasted_iota(jnp.int32, (1, columns), 1) // LANES
    block_sector = block_id // capacity
    block_rank = block_id % capacity
    group = 4
    for t in range(inst_local):
        index_row = jnp.full((1, columns), -1, jnp.int32)
        seen = jnp.zeros((1, columns), jnp.int32)
        for b in range(slots):
            target = jnp.where(b < count_ref[0], matching_ref[t, b], -1)
            hit = block_sector == target
            cells_row = jnp.concatenate([donor_ref[b : b + 1, :]] * (columns // LANES), axis=1)
            index_row = jnp.where(hit & (seen == block_rank), cells_row, index_row)
            seen = seen + jnp.where(hit, 1, 0)
        for first in range(0, columns, part):
            piece = index_row[:, first : first + part]
            high = piece >> 8
            hot = one_hot_rows(piece & (WIDE - 1))

            def step(g, total):
                rows = [
                    source[t, :, pl.ds(pl.multiple_of((g * group + j) * WIDE, WIDE), WIDE)]
                    for j in range(group)
                ]
                picked = jnp.dot(
                    jnp.concatenate(rows, axis=0), hot, preferred_element_type=jnp.float32
                )
                for j in range(group):
                    mine = picked[j * SLOT_ROWS : (j + 1) * SLOT_ROWS]
                    total = total + jnp.where(high == g * group + j, mine, 0.0)
                return total

            total = lax.fori_loop(
                0, cells // WIDE // group, step, jnp.zeros((SLOT_ROWS, part), jnp.float32)
            ).astype(jnp.bfloat16)
            for j in range(part // LANES):
                d, k = divmod(first // LANES + j, capacity)
                send_ref[d, (t * capacity + k) * SLOT_ROWS : (t * capacity + k + 1) * SLOT_ROWS, :] = (
                    total[:, j * LANES : (j + 1) * LANES]
                )


def exchange_kernel(
    sectors, insts, capacity, count_ref, matching_ref, donor_ref, flow_ref, grad_ref, state_ref,
    recv_ref, all_ref, source, send_ref, fs, fr, ss, sr, own,
):
    row = lax.axis_index("row")
    sector = lax.axis_index("sector")
    inst = lax.axis_index("inst")
    barrier = pltpu.get_barrier_semaphore()
    for d in range(sectors):
        pl.semaphore_signal(barrier, inc=1, device_id=(1 - row, d, inst), device_id_type=MESH)
    for step in range(1, insts):
        pl.semaphore_signal(
            barrier, inc=1, device_id=(row, sector, (inst + step) % insts), device_id_type=MESH
        )
    pl.semaphore_wait(barrier, sectors + insts - 1)
    copies = []
    for step in range(1, insts):
        peer = (inst + step) % insts
        copies.append(
            pltpu.make_async_remote_copy(
                src_ref=state_ref,
                dst_ref=all_ref.at[inst],
                send_sem=ss.at[step - 1],
                recv_sem=sr.at[step - 1],
                device_id=(row, sector, peer),
                device_id_type=MESH,
            )
        )
    for copy in copies:
        copy.start()
    mine = pltpu.make_async_copy(state_ref, all_ref.at[inst], own)
    mine.start()
    gather_faces(
        capacity, count_ref, matching_ref, donor_ref, flow_ref, grad_ref, send_ref, source
    )
    for step in range(sectors):
        peer = (sector + step) % sectors
        copy = pltpu.make_async_remote_copy(
            src_ref=send_ref.at[peer],
            dst_ref=recv_ref.at[sector],
            send_sem=fs.at[step],
            recv_sem=fr.at[step],
            device_id=(1 - row, peer, inst),
            device_id_type=MESH,
        )
        copy.start()
        copies.append(copy)
    mine.wait()
    for copy in copies:
        copy.wait()


def update_kernel(
    dmat_ref, freq_ref, recv_ref, weights_ref, offsets_ref, targets_ref, all_ref, state_ref,
    jac_ref, pseudo_ref, out_ref, faces, coupling, stage, out_stage,
):
    inst_local, nvar, cells = state_ref.shape
    sectors, capacity = targets_ref.shape[1:3]
    insts = all_ref.shape[0]
    first_row = lax.axis_index("inst") * inst_local
    rotation = freq_ref[0]
    faces[...] = jnp.zeros_like(faces)
    group = 4
    for t in range(inst_local):
        target_rows = []
        for m in range(sectors):
            for k in range(capacity):
                slot = t * capacity + k
                column = (m * capacity + k) * LANES
                mixed = jnp.dot(
                    recv_ref[m, slot * SLOT_ROWS : (slot + 1) * SLOT_ROWS, :],
                    weights_ref[t, m, k],
                    preferred_element_type=jnp.float32,
                )
                value = mixed[0:nvar]
                for d in range(3):
                    begin = 16 + d * nvar
                    value = value + offsets_ref[t, m, k, d : d + 1, :] * mixed[begin : begin + nvar]
                upper = value.astype(jnp.bfloat16).astype(jnp.float32)
                faces[t, 0:nvar, column : column + LANES] = upper
                faces[t, 8 : 8 + nvar, column : column + LANES] = value - upper
                target_rows.append(targets_ref[t, m, k : k + 1, :])
        target_row = jnp.concatenate(target_rows, axis=1)
        high = target_row >> 8
        hot = one_hot_rows(target_row & (WIDE - 1))

        def spread(g, carry):
            face_values = faces[t]
            rows = [jnp.where(high == g * group + j, face_values, 0.0) for j in range(group)]
            placed = lax.dot_general(
                jnp.concatenate(rows, axis=0).astype(jnp.bfloat16),
                hot,
                (((1,), (1,)), ((), ())),
                preferred_element_type=jnp.float32,
            )
            for j in range(group):
                begin = pl.multiple_of((g * group + j) * WIDE, WIDE)
                coupling[t, :, pl.ds(begin, WIDE)] = (
                    placed[j * 16 : j * 16 + 8] + placed[j * 16 + 8 : j * 16 + 16]
                )
            return carry

        lax.fori_loop(0, cells // WIDE // group, spread, 0)

    chunk = 8 * LANES
    coefs = [
        [dmat_ref[first_row + t, u] * rotation for u in range(insts * inst_local)]
        for t in range(inst_local)
    ]

    def relax(c, carry):
        window = pl.ds(pl.multiple_of(c * chunk, chunk), chunk)
        position = lax.broadcasted_iota(jnp.int32, (inst_local, chunk), 0)
        mixtures = [jnp.zeros((nvar, inst_local, chunk), jnp.float32)] * inst_local
        for i in range(insts):
            segment = all_ref[i, :, :, window].astype(jnp.float32)
            for t in range(inst_local):
                factor = jnp.zeros((inst_local, chunk), jnp.float32)
                for u in range(inst_local):
                    factor = jnp.where(position == u, coefs[t][i * inst_local + u], factor)
                mixtures[t] = mixtures[t] + factor[None] * segment
        for t in range(inst_local):
            jac = jac_ref[t, :, window].astype(jnp.float32)
            flow = state_ref[t, :, window].astype(jnp.float32)
            pseudo = pseudo_ref[t : t + 1, window]
            rest = jnp.sum(mixtures[t], axis=1) - coupling[t, 0:nvar, window]
            for j in range(8):
                lanes = slice(j * LANES, (j + 1) * LANES)
                at = j * STAGE_ROWS
                stage[at : at + nvar * nvar, :] = jac[:, lanes]
                stage[at + 32 : at + 32 + nvar, :] = rest[:, lanes]
                stage[at + 40 : at + 40 + nvar, :] = flow[:, lanes]
                stage[at + 46 : at + 47, :] = pseudo[:, lanes]

            def row(r):
                return stage[pl.ds(r, 8, stride=STAGE_ROWS), :]

            matrix = [[row(v * nvar + w) for w in range(nvar)] for v in range(nvar)]
            base = [row(40 + v) for v in range(nvar)]
            shift = -row(46)

            def apply(start, vector):
                result = []
                for v in range(nvar):
                    acc = start[v]
                    for w in range(nvar):
                        acc = acc + matrix[v][w] * vector[w]
                    result.append(acc)
                return result

            residual = apply([row(32 + v) for v in range(nvar)], base)
            increment = [shift * value for value in residual]
            for sweep in range(SWEEPS):
                increment = [shift * value for value in apply(residual, increment)]
            for v in range(nvar):
                out_stage[pl.ds(v, 8, stride=8), :] = base[v] + increment[v]
            for j in range(8):
                begin = pl.multiple_of(c * chunk + j * LANES, LANES)
                out_ref[t, :, pl.ds(begin, LANES)] = out_stage[j * 8 : j * 8 + nvar, :]
        return carry

    lax.fori_loop(0, cells // chunk, relax, 0)


def body(
    state,
    gradients,
    jacobian,
    pseudo_step,
    frequency,
    donor_cells,
    block_count,
    matching,
    target_cells,
    interp_weights,
    face_offsets,
):
    flow = state[0, 0]
    inst_local, nvar, cells = flow.shape
    sectors = lax.axis_size("sector")
    insts = lax.axis_size("inst")
    capacity = target_cells.shape[4]
    columns = sectors * capacity * LANES
    vmem = pl.BlockSpec(memory_space=pltpu.VMEM)
    smem = pl.BlockSpec(memory_space=pltpu.SMEM)
    hbm = pl.BlockSpec(memory_space=pl.ANY)
    packet = jax.ShapeDtypeStruct((sectors, inst_local * capacity * SLOT_ROWS, LANES), jnp.bfloat16)
    compact = flow.transpose(1, 0, 2)
    recv, everything = pl.pallas_call(
        functools.partial(exchange_kernel, sectors, insts, capacity),
        out_shape=(packet, jax.ShapeDtypeStruct((insts,) + compact.shape, flow.dtype)),
        in_specs=[smem, smem, vmem, vmem, vmem, hbm],
        out_specs=(hbm, hbm),
        scratch_shapes=[
            pltpu.VMEM((inst_local, SLOT_ROWS, cells), jnp.bfloat16),
            pltpu.VMEM(packet.shape, packet.dtype),
            pltpu.SemaphoreType.DMA((sectors,)),
            pltpu.SemaphoreType.DMA((sectors,)),
            pltpu.SemaphoreType.DMA((insts - 1,)),
            pltpu.SemaphoreType.DMA((insts - 1,)),
            pltpu.SemaphoreType.DMA,
        ],
        compiler_params=pltpu.CompilerParams(
            collective_id=0, has_side_effects=True, vmem_limit_bytes=VMEM_LIMIT
        ),
    )(block_count.reshape(1), matching[0, 0], donor_cells[0, 0], flow, gradients[0, 0], compact)
    dmat = jnp.asarray(spectral_matrix(inst_local * insts))
    result = pl.pallas_call(
        update_kernel,
        out_shape=jax.ShapeDtypeStruct(flow.shape, jnp.float32),
        in_specs=[smem, smem] + [vmem] * 8,
        out_specs=vmem,
        scratch_shapes=[
            pltpu.VMEM((inst_local, 16, columns), jnp.float32),
            pltpu.VMEM((inst_local, 8, cells), jnp.float32),
            pltpu.VMEM((8 * STAGE_ROWS, LANES), jnp.float32),
            pltpu.VMEM((64, LANES), jnp.float32),
        ],
        compiler_params=pltpu.CompilerParams(vmem_limit_bytes=VMEM_LIMIT),
    )(
        dmat,
        frequency,
        recv,
        interp_weights[0, 0],
        face_offsets[0, 0],
        target_cells[0, 0],
        everything,
        flow,
        jacobian[0, 0],
        pseudo_step[0, 0],
    )
    return result[None, None]


def solution(mesh):
    placed = (
        P("row", "sector", "inst", None, None),
        P("row", "sector", "inst", None, None),
        P("row", "sector", "inst", None, None),
        P("row", "sector", "inst", None),
        P("row"),
        P("row", "sector", None, None),
        P("row", "sector"),
        P("row", "sector", "inst", None),
        P("row", "sector", "inst", None, None, None),
        P("row", "sector", "inst", None, None, None, None),
        P("row", "sector", "inst", None, None, None, None),
    )
    return jax.shard_map(
        body,
        mesh=mesh,
        in_specs=placed,
        out_specs=P("row", "sector", "inst", None, None),
        check_vma=False,
    )
```

```python
import functools
import math

import jax
import jax.numpy as jnp
import numpy as np
from jax import lax
from jax.experimental import pallas as pl
from jax.experimental.pallas import tpu as pltpu
from jax.sharding import PartitionSpec as P

SWEEPS = 6
LANES = 128
WIDE = 256
SLOT_ROWS = 32
STAGE_ROWS = 48
MESH = pl.DeviceIdType.MESH
VMEM_LIMIT = 48 * 1024 * 1024


def spectral_matrix(period):
    index = np.arange(period)
    gap = index[:, None] - index[None, :]
    safe_gap = np.where(gap == 0, 1, gap)
    angle = safe_gap * (math.pi / period)
    entry = 0.5 * (1 - 2 * (np.abs(gap) % 2)) * np.cos(angle) / np.sin(angle)
    return np.where(gap == 0, 0.0, entry).astype(np.float32)


def one_hot_rows(index_row):
    rows = lax.broadcasted_iota(jnp.int32, (WIDE, index_row.shape[1]), 0)
    return jnp.where(rows == index_row, 1.0, 0.0).astype(jnp.bfloat16)


def gather_faces(capacity, count_ref, matching_ref, donor_ref, state_ref, grad_ref, send_ref, source):
    inst_local, nvar, cells = state_ref.shape
    nslope = grad_ref.shape[1]
    slots = donor_ref.shape[0]
    sectors = send_ref.shape[0]
    columns = sectors * capacity * LANES
    part = min(columns, 1024)
    source[...] = jnp.zeros_like(source)
    for t in range(inst_local):
        source[t, 0:nvar, :] = state_ref[t]
        source[t, 16 : 16 + nslope, :] = grad_ref[t]
    block_id = lax.broadcasted_iota(jnp.int32, (1, columns), 1) // LANES
    block_sector = block_id // capacity
    block_rank = block_id % capacity
    group = 4
    for t in range(inst_local):
        index_row = jnp.full((1, columns), -1, jnp.int32)
        seen = jnp.zeros((1, columns), jnp.int32)
        for b in range(slots):
            target = jnp.where(b < count_ref[0], matching_ref[t, b], -1)
            hit = block_sector == target
            cells_row = jnp.concatenate([donor_ref[b : b + 1, :]] * (columns // LANES), axis=1)
            index_row = jnp.where(hit & (seen == block_rank), cells_row, index_row)
            seen = seen + jnp.where(hit, 1, 0)
        for first in range(0, columns, part):
            piece = index_row[:, first : first + part]
            high = piece >> 8
            hot = one_hot_rows(piece & (WIDE - 1))

            def step(g, total):
                rows = [
                    source[t, :, pl.ds(pl.multiple_of((g * group + j) * WIDE, WIDE), WIDE)]
                    for j in range(group)
                ]
                picked = jnp.dot(
                    jnp.concatenate(rows, axis=0), hot, preferred_element_type=jnp.float32
                )
                for j in range(group):
                    mine = picked[j * SLOT_ROWS : (j + 1) * SLOT_ROWS]
                    total = total + jnp.where(high == g * group + j, mine, 0.0)
                return total

            total = lax.fori_loop(
                0, cells // WIDE // group, step, jnp.zeros((SLOT_ROWS, part), jnp.float32)
            ).astype(jnp.bfloat16)
            for j in range(part // LANES):
                d, k = divmod(first // LANES + j, capacity)
                send_ref[d, (t * capacity + k) * SLOT_ROWS : (t * capacity + k + 1) * SLOT_ROWS, :] = (
                    total[:, j * LANES : (j + 1) * LANES]
                )


def couple_faces(nvar, recv_ref, weights_ref, offsets_ref, targets_ref, faces, coupling):
    inst_local, sectors, capacity = targets_ref.shape[:3]
    cells = coupling.shape[2]
    faces[...] = jnp.zeros_like(faces)
    group = 4
    for t in range(inst_local):
        target_rows = []
        for m in range(sectors):
            for k in range(capacity):
                slot = t * capacity + k
                column = (m * capacity + k) * LANES
                mixed = jnp.dot(
                    recv_ref[m, slot * SLOT_ROWS : (slot + 1) * SLOT_ROWS, :],
                    weights_ref[t, m, k],
                    preferred_element_type=jnp.float32,
                )
                value = mixed[0:nvar]
                for d in range(3):
                    begin = 16 + d * nvar
                    value = value + offsets_ref[t, m, k, d : d + 1, :] * mixed[begin : begin + nvar]
                upper = value.astype(jnp.bfloat16).astype(jnp.float32)
                faces[t, 0:nvar, column : column + LANES] = upper
                faces[t, 8 : 8 + nvar, column : column + LANES] = value - upper
                target_rows.append(targets_ref[t, m, k : k + 1, :])
        target_row = jnp.concatenate(target_rows, axis=1)
        high = target_row >> 8
        hot = one_hot_rows(target_row & (WIDE - 1))

        def spread(g, carry):
            face_values = faces[t]
            rows = [jnp.where(high == g * group + j, face_values, 0.0) for j in range(group)]
            placed = lax.dot_general(
                jnp.concatenate(rows, axis=0).astype(jnp.bfloat16),
                hot,
                (((1,), (1,)), ((), ())),
                preferred_element_type=jnp.float32,
            )
            for j in range(group):
                begin = pl.multiple_of((g * group + j) * WIDE, WIDE)
                coupling[t, :, pl.ds(begin, WIDE)] = (
                    placed[j * 16 : j * 16 + 8] + placed[j * 16 + 8 : j * 16 + 16]
                )
            return carry

        lax.fori_loop(0, cells // WIDE // group, spread, 0)


def exchange_kernel(
    sectors, insts, capacity, count_ref, matching_ref, donor_ref, flow_ref, grad_ref, weights_ref,
    offsets_ref, targets_ref, state_ref, coupling, all_ref, source, send_ref, recv_ref, faces,
    fs, fr, ss, sr, own,
):
    row = lax.axis_index("row")
    sector = lax.axis_index("sector")
    inst = lax.axis_index("inst")
    barrier = pltpu.get_barrier_semaphore()
    for d in range(sectors):
        pl.semaphore_signal(barrier, inc=1, device_id=(1 - row, d, inst), device_id_type=MESH)
    for step in range(1, insts):
        pl.semaphore_signal(
            barrier, inc=1, device_id=(row, sector, (inst + step) % insts), device_id_type=MESH
        )
    pl.semaphore_wait(barrier, sectors + insts - 1)
    copies = []
    for step in range(1, insts):
        peer = (inst + step) % insts
        copies.append(
            pltpu.make_async_remote_copy(
                src_ref=state_ref,
                dst_ref=all_ref.at[inst],
                send_sem=ss.at[step - 1],
                recv_sem=sr.at[step - 1],
                device_id=(row, sector, peer),
                device_id_type=MESH,
            )
        )
    for copy in copies:
        copy.start()
    mine = pltpu.make_async_copy(state_ref, all_ref.at[inst], own)
    mine.start()
    gather_faces(
        capacity, count_ref, matching_ref, donor_ref, flow_ref, grad_ref, send_ref, source
    )
    arrivals = []
    for step in range(sectors):
        peer = (sector + step) % sectors
        copy = pltpu.make_async_remote_copy(
            src_ref=send_ref.at[peer],
            dst_ref=recv_ref.at[sector],
            send_sem=fs.at[step],
            recv_sem=fr.at[step],
            device_id=(1 - row, peer, inst),
            device_id_type=MESH,
        )
        copy.start()
        arrivals.append(copy)
    for copy in arrivals:
        copy.wait()
    couple_faces(
        flow_ref.shape[1], recv_ref, weights_ref, offsets_ref, targets_ref, faces, coupling
    )
    mine.wait()
    for copy in copies:
        copy.wait()


def update_kernel(
    dmat_ref, freq_ref, coupling, all_ref, state_ref, jac_ref, pseudo_ref, out_ref, stage, out_stage
):
    inst_local, nvar, cells = state_ref.shape
    insts = all_ref.shape[0]
    first_row = lax.axis_index("inst") * inst_local
    rotation = freq_ref[0]
    chunk = 8 * LANES
    coefs = [
        [dmat_ref[first_row + t, u] * rotation for u in range(insts * inst_local)]
        for t in range(inst_local)
    ]

    def relax(c, carry):
        window = pl.ds(pl.multiple_of(c * chunk, chunk), chunk)
        position = lax.broadcasted_iota(jnp.int32, (inst_local, chunk), 0)
        mixtures = [jnp.zeros((nvar, inst_local, chunk), jnp.float32)] * inst_local
        for i in range(insts):
            segment = all_ref[i, :, :, window].astype(jnp.float32)
            for t in range(inst_local):
                factor = jnp.zeros((inst_local, chunk), jnp.float32)
                for u in range(inst_local):
                    factor = jnp.where(position == u, coefs[t][i * inst_local + u], factor)
                mixtures[t] = mixtures[t] + factor[None] * segment
        for t in range(inst_local):
            jac = jac_ref[t, :, window].astype(jnp.float32)
            flow = state_ref[t, :, window].astype(jnp.float32)
            pseudo = pseudo_ref[t : t + 1, window]
            rest = jnp.sum(mixtures[t], axis=1) - coupling[t, 0:nvar, window]
            for j in range(8):
                lanes = slice(j * LANES, (j + 1) * LANES)
                at = j * STAGE_ROWS
                stage[at : at + nvar * nvar, :] = jac[:, lanes]
                stage[at + 32 : at + 32 + nvar, :] = rest[:, lanes]
                stage[at + 40 : at + 40 + nvar, :] = flow[:, lanes]
                stage[at + 46 : at + 47, :] = pseudo[:, lanes]

            def row(r):
                return stage[pl.ds(r, 8, stride=STAGE_ROWS), :]

            matrix = [[row(v * nvar + w) for w in range(nvar)] for v in range(nvar)]
            base = [row(40 + v) for v in range(nvar)]
            shift = -row(46)

            def apply(start, vector):
                result = []
                for v in range(nvar):
                    acc = start[v]
                    for w in range(nvar):
                        acc = acc + matrix[v][w] * vector[w]
                    result.append(acc)
                return result

            residual = apply([row(32 + v) for v in range(nvar)], base)
            increment = [shift * value for value in residual]
            for sweep in range(SWEEPS):
                increment = [shift * value for value in apply(residual, increment)]
            for v in range(nvar):
                out_stage[pl.ds(v, 8, stride=8), :] = base[v] + increment[v]
            for j in range(8):
                begin = pl.multiple_of(c * chunk + j * LANES, LANES)
                out_ref[t, :, pl.ds(begin, LANES)] = out_stage[j * 8 : j * 8 + nvar, :]
        return carry

    lax.fori_loop(0, cells // chunk, relax, 0)


def body(
    state,
    gradients,
    jacobian,
    pseudo_step,
    frequency,
    donor_cells,
    block_count,
    matching,
    target_cells,
    interp_weights,
    face_offsets,
):
    flow = state[0, 0]
    inst_local, nvar, cells = flow.shape
    sectors = lax.axis_size("sector")
    insts = lax.axis_size("inst")
    capacity = target_cells.shape[4]
    columns = sectors * capacity * LANES
    vmem = pl.BlockSpec(memory_space=pltpu.VMEM)
    smem = pl.BlockSpec(memory_space=pltpu.SMEM)
    hbm = pl.BlockSpec(memory_space=pl.ANY)
    packet = jax.ShapeDtypeStruct((sectors, inst_local * capacity * SLOT_ROWS, LANES), jnp.bfloat16)
    compact = flow.transpose(1, 0, 2)
    coupling, everything = pl.pallas_call(
        functools.partial(exchange_kernel, sectors, insts, capacity),
        out_shape=(jax.ShapeDtypeStruct((inst_local, 8, cells), jnp.float32), jax.ShapeDtypeStruct((insts,) + compact.shape, flow.dtype)),
        in_specs=[smem, smem] + [vmem] * 6 + [hbm],
        out_specs=(vmem, hbm),
        scratch_shapes=[
            pltpu.VMEM((inst_local, SLOT_ROWS, cells), jnp.bfloat16),
            pltpu.VMEM(packet.shape, packet.dtype),
            pltpu.VMEM(packet.shape, packet.dtype),
            pltpu.VMEM((inst_local, 16, columns), jnp.float32),
            pltpu.SemaphoreType.DMA((sectors,)),
            pltpu.SemaphoreType.DMA((sectors,)),
            pltpu.SemaphoreType.DMA((insts - 1,)),
            pltpu.SemaphoreType.DMA((insts - 1,)),
            pltpu.SemaphoreType.DMA,
        ],
        compiler_params=pltpu.CompilerParams(
            collective_id=0, has_side_effects=True, vmem_limit_bytes=VMEM_LIMIT
        ),
    )(block_count.reshape(1), matching[0, 0], donor_cells[0, 0], flow, gradients[0, 0],
      interp_weights[0, 0], face_offsets[0, 0], target_cells[0, 0], compact)
    dmat = jnp.asarray(spectral_matrix(inst_local * insts))
    result = pl.pallas_call(
        update_kernel,
        out_shape=jax.ShapeDtypeStruct(flow.shape, jnp.float32),
        in_specs=[smem, smem] + [vmem] * 5,
        out_specs=vmem,
        scratch_shapes=[
            pltpu.VMEM((8 * STAGE_ROWS, LANES), jnp.float32),
            pltpu.VMEM((64, LANES), jnp.float32),
        ],
        compiler_params=pltpu.CompilerParams(vmem_limit_bytes=VMEM_LIMIT),
    )(
        dmat,
        frequency,
        coupling,
        everything,
        flow,
        jacobian[0, 0],
        pseudo_step[0, 0],
    )
    return result[None, None]


def solution(mesh):
    placed = (
        P("row", "sector", "inst", None, None),
        P("row", "sector", "inst", None, None),
        P("row", "sector", "inst", None, None),
        P("row", "sector", "inst", None),
        P("row"),
        P("row", "sector", None, None),
        P("row", "sector"),
        P("row", "sector", "inst", None),
        P("row", "sector", "inst", None, None, None),
        P("row", "sector", "inst", None, None, None, None),
        P("row", "sector", "inst", None, None, None, None),
    )
    return jax.shard_map(
        body,
        mesh=mesh,
        in_specs=placed,
        out_specs=P("row", "sector", "inst", None, None),
        check_vma=False,
    )
```

```python
import functools
import math

import jax
import jax.numpy as jnp
import numpy as np
from jax import lax
from jax.experimental import pallas as pl
from jax.experimental.pallas import tpu as pltpu
from jax.sharding import PartitionSpec as P

SWEEPS = 6
LANES = 128
WIDE = 256
SLOT_ROWS = 32
STAGE_ROWS = 48
MESH = pl.DeviceIdType.MESH
VMEM_LIMIT = 48 * 1024 * 1024


def spectral_matrix(period):
    index = np.arange(period)
    gap = index[:, None] - index[None, :]
    safe_gap = np.where(gap == 0, 1, gap)
    angle = safe_gap * (math.pi / period)
    entry = 0.5 * (1 - 2 * (np.abs(gap) % 2)) * np.cos(angle) / np.sin(angle)
    return np.where(gap == 0, 0.0, entry).astype(np.float32)


def one_hot_rows(index_row):
    rows = lax.broadcasted_iota(jnp.int32, (WIDE, index_row.shape[1]), 0)
    return jnp.where(rows == index_row, 1.0, 0.0).astype(jnp.bfloat16)


def gather_faces(capacity, count_ref, matching_ref, donor_ref, state_ref, grad_ref, send_ref, source):
    inst_local, nvar, cells = state_ref.shape
    nslope = grad_ref.shape[1]
    slots = donor_ref.shape[0]
    sectors = send_ref.shape[0]
    columns = sectors * capacity * LANES
    part = min(columns, 1024)
    source[...] = jnp.zeros_like(source)
    for t in range(inst_local):
        source[t, 0:nvar, :] = state_ref[t]
        source[t, 16 : 16 + nslope, :] = grad_ref[t]
    block_id = lax.broadcasted_iota(jnp.int32, (1, columns), 1) // LANES
    block_sector = block_id // capacity
    block_rank = block_id % capacity
    group = 4
    for t in range(inst_local):
        index_row = jnp.full((1, columns), -1, jnp.int32)
        seen = jnp.zeros((1, columns), jnp.int32)
        for b in range(slots):
            target = jnp.where(b < count_ref[0], matching_ref[t, b], -1)
            hit = block_sector == target
            cells_row = jnp.concatenate([donor_ref[b : b + 1, :]] * (columns // LANES), axis=1)
            index_row = jnp.where(hit & (seen == block_rank), cells_row, index_row)
            seen = seen + jnp.where(hit, 1, 0)
        for first in range(0, columns, part):
            piece = index_row[:, first : first + part]
            high = piece >> 8
            hot = one_hot_rows(piece & (WIDE - 1))

            def step(g, total):
                rows = [
                    source[t, :, pl.ds(pl.multiple_of((g * group + j) * WIDE, WIDE), WIDE)]
                    for j in range(group)
                ]
                picked = jnp.dot(
                    jnp.concatenate(rows, axis=0), hot, preferred_element_type=jnp.float32
                )
                for j in range(group):
                    mine = picked[j * SLOT_ROWS : (j + 1) * SLOT_ROWS]
                    total = total + jnp.where(high == g * group + j, mine, 0.0)
                return total

            total = lax.fori_loop(
                0, cells // WIDE // group, step, jnp.zeros((SLOT_ROWS, part), jnp.float32)
            ).astype(jnp.bfloat16)
            for j in range(part // LANES):
                d, k = divmod(first // LANES + j, capacity)
                send_ref[d, (t * capacity + k) * SLOT_ROWS : (t * capacity + k + 1) * SLOT_ROWS, :] = (
                    total[:, j * LANES : (j + 1) * LANES]
                )


def couple_faces(nvar, recv_ref, weights_ref, offsets_ref, targets_ref, faces, coupling):
    inst_local, sectors, capacity = targets_ref.shape[:3]
    cells = coupling.shape[2]
    faces[...] = jnp.zeros_like(faces)
    group = 4
    for t in range(inst_local):
        target_rows = []
        for m in range(sectors):
            for k in range(capacity):
                slot = t * capacity + k
                column = (m * capacity + k) * LANES
                mixed = jnp.dot(
                    recv_ref[m, slot * SLOT_ROWS : (slot + 1) * SLOT_ROWS, :],
                    weights_ref[t, m, k],
                    preferred_element_type=jnp.float32,
                )
                value = mixed[0:nvar]
                for d in range(3):
                    begin = 16 + d * nvar
                    value = value + offsets_ref[t, m, k, d : d + 1, :] * mixed[begin : begin + nvar]
                upper = value.astype(jnp.bfloat16).astype(jnp.float32)
                faces[t, 0:nvar, column : column + LANES] = upper
                faces[t, 8 : 8 + nvar, column : column + LANES] = value - upper
                target_rows.append(targets_ref[t, m, k : k + 1, :])
        target_row = jnp.concatenate(target_rows, axis=1)
        high = target_row >> 8
        hot = one_hot_rows(target_row & (WIDE - 1))

        def spread(g, carry):
            face_values = faces[t]
            rows = [jnp.where(high == g * group + j, face_values, 0.0) for j in range(group)]
            placed = lax.dot_general(
                jnp.concatenate(rows, axis=0).astype(jnp.bfloat16),
                hot,
                (((1,), (1,)), ((), ())),
                preferred_element_type=jnp.float32,
            )
            for j in range(group):
                begin = pl.multiple_of((g * group + j) * WIDE, WIDE)
                coupling[t, :, pl.ds(begin, WIDE)] = (
                    placed[j * 16 : j * 16 + 8] + placed[j * 16 + 8 : j * 16 + 16]
                )
            return carry

        lax.fori_loop(0, cells // WIDE // group, spread, 0)


def exchange_kernel(
    sectors, insts, capacity, count_ref, matching_ref, donor_ref, flow_ref, grad_ref, weights_ref,
    offsets_ref, targets_ref, state_ref, coupling, all_ref, source, send_ref, recv_ref, faces,
    fs, fr, ss, sr, own,
):
    row = lax.axis_index("row")
    sector = lax.axis_index("sector")
    inst = lax.axis_index("inst")
    barrier = pltpu.get_barrier_semaphore()
    for d in range(sectors):
        pl.semaphore_signal(barrier, inc=1, device_id=(1 - row, d, inst), device_id_type=MESH)
    for step in range(1, insts):
        pl.semaphore_signal(
            barrier, inc=1, device_id=(row, sector, (inst + step) % insts), device_id_type=MESH
        )
    pl.semaphore_wait(barrier, sectors + insts - 1)

    def hop(side, step):
        shift = 1 - 2 * side
        origin = jnp.clip(inst - shift * step, 0, insts - 1)
        slot = side * (insts - 1) + step
        return pltpu.make_async_remote_copy(
            src_ref=state_ref if step == 0 else all_ref.at[origin],
            dst_ref=all_ref.at[origin],
            send_sem=ss.at[slot],
            recv_sem=sr.at[slot],
            device_id=(row, sector, jnp.clip(inst + shift, 0, insts - 1)),
            device_id_type=MESH,
        )

    def behind(side):
        return inst if side == 0 else insts - 1 - inst

    def forward(step):
        for side in range(2):
            if step > 0:
                pl.when(behind(side) >= step)(lambda: hop(side, step - 1).wait_recv())
            if step < insts - 1:
                sends = (behind(side) >= step) & (behind(side) < insts - 1)
                pl.when(sends)(lambda: hop(side, step).start())

    forward(0)
    mine = pltpu.make_async_copy(state_ref, all_ref.at[inst], own)
    mine.start()
    gather_faces(
        capacity, count_ref, matching_ref, donor_ref, flow_ref, grad_ref, send_ref, source
    )
    arrivals = []
    for step in range(sectors):
        peer = (sector + step) % sectors
        copy = pltpu.make_async_remote_copy(
            src_ref=send_ref.at[peer],
            dst_ref=recv_ref.at[sector],
            send_sem=fs.at[step],
            recv_sem=fr.at[step],
            device_id=(1 - row, peer, inst),
            device_id_type=MESH,
        )
        copy.start()
        arrivals.append(copy)
    forward(1)
    for copy in arrivals:
        copy.wait()
    couple_faces(
        flow_ref.shape[1], recv_ref, weights_ref, offsets_ref, targets_ref, faces, coupling
    )
    mine.wait()
    for step in range(2, insts):
        forward(step)
    for side in range(2):
        for step in range(insts - 1):
            sends = (behind(side) >= step) & (behind(side) < insts - 1)
            pl.when(sends)(lambda: hop(side, step).wait_send())


def update_kernel(
    dmat_ref, freq_ref, coupling, all_ref, state_ref, jac_ref, pseudo_ref, out_ref, stage, out_stage
):
    inst_local, nvar, cells = state_ref.shape
    insts = all_ref.shape[0]
    first_row = lax.axis_index("inst") * inst_local
    rotation = freq_ref[0]
    chunk = 8 * LANES
    coefs = [
        [dmat_ref[first_row + t, u] * rotation for u in range(insts * inst_local)]
        for t in range(inst_local)
    ]

    def relax(c, carry):
        window = pl.ds(pl.multiple_of(c * chunk, chunk), chunk)
        position = lax.broadcasted_iota(jnp.int32, (inst_local, chunk), 0)
        mixtures = [jnp.zeros((nvar, inst_local, chunk), jnp.float32)] * inst_local
        for i in range(insts):
            segment = all_ref[i, :, :, window].astype(jnp.float32)
            for t in range(inst_local):
                factor = jnp.zeros((inst_local, chunk), jnp.float32)
                for u in range(inst_local):
                    factor = jnp.where(position == u, coefs[t][i * inst_local + u], factor)
                mixtures[t] = mixtures[t] + factor[None] * segment
        for t in range(inst_local):
            jac = jac_ref[t, :, window].astype(jnp.float32)
            flow = state_ref[t, :, window].astype(jnp.float32)
            pseudo = pseudo_ref[t : t + 1, window]
            rest = jnp.sum(mixtures[t], axis=1) - coupling[t, 0:nvar, window]
            for j in range(8):
                lanes = slice(j * LANES, (j + 1) * LANES)
                at = j * STAGE_ROWS
                stage[at : at + nvar * nvar, :] = jac[:, lanes]
                stage[at + 32 : at + 32 + nvar, :] = rest[:, lanes]
                stage[at + 40 : at + 40 + nvar, :] = flow[:, lanes]
                stage[at + 46 : at + 47, :] = pseudo[:, lanes]

            def row(r):
                return stage[pl.ds(r, 8, stride=STAGE_ROWS), :]

            matrix = [[row(v * nvar + w) for w in range(nvar)] for v in range(nvar)]
            base = [row(40 + v) for v in range(nvar)]
            shift = -row(46)

            def apply(start, vector):
                result = []
                for v in range(nvar):
                    acc = start[v]
                    for w in range(nvar):
                        acc = acc + matrix[v][w] * vector[w]
                    result.append(acc)
                return result

            residual = apply([row(32 + v) for v in range(nvar)], base)
            increment = [shift * value for value in residual]
            for sweep in range(SWEEPS):
                increment = [shift * value for value in apply(residual, increment)]
            for v in range(nvar):
                out_stage[pl.ds(v, 8, stride=8), :] = base[v] + increment[v]
            for j in range(8):
                begin = pl.multiple_of(c * chunk + j * LANES, LANES)
                out_ref[t, :, pl.ds(begin, LANES)] = out_stage[j * 8 : j * 8 + nvar, :]
        return carry

    lax.fori_loop(0, cells // chunk, relax, 0)


def body(
    state,
    gradients,
    jacobian,
    pseudo_step,
    frequency,
    donor_cells,
    block_count,
    matching,
    target_cells,
    interp_weights,
    face_offsets,
):
    flow = state[0, 0]
    inst_local, nvar, cells = flow.shape
    sectors = lax.axis_size("sector")
    insts = lax.axis_size("inst")
    capacity = target_cells.shape[4]
    columns = sectors * capacity * LANES
    vmem = pl.BlockSpec(memory_space=pltpu.VMEM)
    smem = pl.BlockSpec(memory_space=pltpu.SMEM)
    hbm = pl.BlockSpec(memory_space=pl.ANY)
    packet = jax.ShapeDtypeStruct((sectors, inst_local * capacity * SLOT_ROWS, LANES), jnp.bfloat16)
    compact = flow.transpose(1, 0, 2)
    coupling, everything = pl.pallas_call(
        functools.partial(exchange_kernel, sectors, insts, capacity),
        out_shape=(jax.ShapeDtypeStruct((inst_local, 8, cells), jnp.float32), jax.ShapeDtypeStruct((insts,) + compact.shape, flow.dtype)),
        in_specs=[smem, smem] + [vmem] * 6 + [hbm],
        out_specs=(vmem, hbm),
        scratch_shapes=[
            pltpu.VMEM((inst_local, SLOT_ROWS, cells), jnp.bfloat16),
            pltpu.VMEM(packet.shape, packet.dtype),
            pltpu.VMEM(packet.shape, packet.dtype),
            pltpu.VMEM((inst_local, 16, columns), jnp.float32),
            pltpu.SemaphoreType.DMA((sectors,)),
            pltpu.SemaphoreType.DMA((sectors,)),
            pltpu.SemaphoreType.DMA((2 * (insts - 1),)),
            pltpu.SemaphoreType.DMA((2 * (insts - 1),)),
            pltpu.SemaphoreType.DMA,
        ],
        compiler_params=pltpu.CompilerParams(
            collective_id=0, has_side_effects=True, vmem_limit_bytes=VMEM_LIMIT
        ),
    )(block_count.reshape(1), matching[0, 0], donor_cells[0, 0], flow, gradients[0, 0],
      interp_weights[0, 0], face_offsets[0, 0], target_cells[0, 0], compact)
    dmat = jnp.asarray(spectral_matrix(inst_local * insts))
    result = pl.pallas_call(
        update_kernel,
        out_shape=jax.ShapeDtypeStruct(flow.shape, jnp.float32),
        in_specs=[smem, smem] + [vmem] * 5,
        out_specs=vmem,
        scratch_shapes=[
            pltpu.VMEM((8 * STAGE_ROWS, LANES), jnp.float32),
            pltpu.VMEM((64, LANES), jnp.float32),
        ],
        compiler_params=pltpu.CompilerParams(vmem_limit_bytes=VMEM_LIMIT),
    )(
        dmat,
        frequency,
        coupling,
        everything,
        flow,
        jacobian[0, 0],
        pseudo_step[0, 0],
    )
    return result[None, None]


def solution(mesh):
    placed = (
        P("row", "sector", "inst", None, None),
        P("row", "sector", "inst", None, None),
        P("row", "sector", "inst", None, None),
        P("row", "sector", "inst", None),
        P("row"),
        P("row", "sector", None, None),
        P("row", "sector"),
        P("row", "sector", "inst", None),
        P("row", "sector", "inst", None, None, None),
        P("row", "sector", "inst", None, None, None, None),
        P("row", "sector", "inst", None, None, None, None),
    )
    return jax.shard_map(
        body,
        mesh=mesh,
        in_specs=placed,
        out_specs=P("row", "sector", "inst", None, None),
        check_vma=False,
    )
```
